128 devices in a mesh: grp: 4 (over y), ep: 32 (over z, x, core).
Axes of the slice: x: 4, y: 4, z: 4, core: 2. Of those that a mesh axis runs over, the one named last changes fastest.
Arguments:
- hidden: bfloat16 [1024, 2, 3584], P(('grp', 'ep')), may hold values from -6 to 6
- norm_gain: float32 [3584], replicated, may hold values from 0.5 to 1.5
- route_ids: int32 [1024, 2, 8], P(('grp', 'ep')), may hold values from 0 to 127, all different within a row; in each aligned block of 16 rows (0 to 15, 16 to 31, ..., all dimensions but the last counted through in order) at most 2 rows name the same one
- gate_weights: float32 [1024, 2, 8], P(('grp', 'ep')), may hold values from 0.1 to 0.5
- w_gate: bfloat16 [128, 3584, 1024], P(('grp', 'ep')), may hold values from -0.09375 to 0.09375
- w_up: bfloat16 [128, 3584, 1024], P(('grp', 'ep')), may hold values from -0.09375 to 0.09375
- w_down: bfloat16 [128, 1024, 3584], P(('grp', 'ep')), may hold values from -0.1875 to 0.1875
Outputs:
- moe_out: bfloat16 [1024, 2, 3584], P(('grp', 'ep'))
The draws below stay inside these ranges and needn't reach their ends.
Inputs may be any that keep to these rules, and one draw needn't show every extreme that they name: `route_ids`: each row names 8 distinct experts; among the 16 rows of one device (all steps together) no expert is named more than 2 times, a bound that some block reaches.
All inputs are finite; a program needn't handle non-finite values.
Results may differ from the reference program's by a relative error of at most 0.0071.
Values may be sent and summed in bfloat16 or wider, within the bound.
A program may use at most 128 MiB of HBM per device.

```python
import math
import jax
import jax.numpy as jnp
import numpy as np
from jax import lax

D = 3584
FFH = 1024
TOPK = 8
STEPS = 2
ROWS_DEV = 8
TOKENS = 1024
EXPERTS = 128
MOST = 2
N_GRP = 4
N_EP = 32


def steps_of(stream_key, dims, shards, least, largest):
    def one(dim, blocks):
        steps = jax.random.uniform(jax.random.fold_in(jax.random.fold_in(stream_key, 6), dim), (blocks,), jnp.float32, least / len(shards), largest / len(shards))
        return jnp.repeat(jnp.exp(steps), dims[dim] // blocks).reshape((-1,) + (1,) * (len(dims) - dim - 1))

    gain = one(*shards[0])
    for cut in shards[1:]:
        gain = gain * one(*cut)
    return gain


def assign_block(own_key, own, number, rows, number_of, top, bound, lean):
    ranking = jax.random.permutation(own_key, number_of)
    crowded, common = shares(number_of, rows * top, bound, lean, True), shares(number_of, rows * top, bound, lean, False)
    places = jnp.arange(number_of)

    def named(tallies, turn):
        used = int((tallies > 0).sum())
        fixed = max(1, used // 4)
        moved = fixed + (places - fixed + turn * (used - fixed)) % max(1, number_of - fixed)
        return jnp.zeros((number_of,), jnp.int32).at[ranking[jnp.where(places < fixed, places, moved)]].set(jnp.asarray(tallies, jnp.int32))

    tallies = jnp.where(number % 4 == 0, named(crowded, number // 4), named(common, number - number // 4 - 1))
    mixed = jax.random.permutation(jax.random.fold_in(own, 3), number_of)
    donor, receiver = mixed[0:number_of // 2 * 2:2], mixed[1:number_of // 2 * 2:2]
    margin = jnp.minimum(tallies[donor] - 1, bound - tallies[receiver]) // 2
    margin = jnp.where((donor == ranking[0]) | (receiver == ranking[0]) | (tallies[receiver] == 0), 0, jnp.maximum(margin, 0))
    moved = jax.random.randint(jax.random.fold_in(own, 4), (number_of // 2,), 0, 1 << 20) % (margin + 1)
    tallies = tallies.at[donor].add(-moved).at[receiver].add(moved)
    labels = jnp.searchsorted(jnp.cumsum(tallies), jnp.arange(rows * top), side="right").astype(jnp.int32)
    listing = labels.reshape(top, rows).T
    listing = listing[jax.random.permutation(jax.random.fold_in(own, 1), rows)]
    turn = jax.random.randint(jax.random.fold_in(own, 2), (rows, 1), 0, top)
    return jnp.take_along_axis(listing, (jnp.arange(top)[None, :] + turn) % top, axis=1)


def shares(number_of, total, limit, slope, full):
    portions = [(1 << 20) // math.isqrt(rank ** slope) + 1 for rank in range(1, number_of + 1)]
    largest = limit if full else min(limit, max(-(-total // number_of), total * portions[0] // sum(portions)))
    least = 1 if total - largest >= number_of - 1 else 0
    holding, spare = [largest] + [least] * (number_of - 1), total - largest - least * (number_of - 1)
    while spare > 0:
        movable = [i for i in range(1, number_of) if holding[i] < largest] or [i for i in range(1, number_of) if holding[i] < limit]
        mass, remaining = sum([portions[i] for i in movable]), spare
        for i in movable:
            more = min(limit - holding[i], max(1, remaining * portions[i] // mass), spare)
            holding[i] = holding[i] + more
            spare = spare - more
    return np.array(holding)


def noise(rng, extent, deviation, limit, cuts=(), kind=jnp.bfloat16):
    loudness = steps_of(rng, extent, cuts, -0.22, 0.18) if cuts else 1.0
    array = jax.random.normal(rng, extent, jnp.float32) * deviation * loudness
    return jnp.minimum(jnp.maximum(array, -limit), limit).astype(kind)


def setup_inputs(seed: int = 0) -> dict:
    keys = jax.random.split(jax.random.key(seed), 8)
    hidden = noise(keys[0], (TOKENS, STEPS, D), 1.0, 6.0, ((0, 128),))
    norm_gain = jnp.clip(1.0 + 0.1 * jax.random.normal(keys[1], (D,), jnp.float32), 0.5, 1.5)
    route_ids_keys = jax.random.split(jax.random.fold_in(keys[2], 1), TOKENS * STEPS // (ROWS_DEV * STEPS))
    route_ids_turns = jax.random.permutation(jax.random.fold_in(keys[2], 3), TOKENS * STEPS // (ROWS_DEV * STEPS))
    route_ids = jax.vmap(lambda own, number: assign_block(jax.random.fold_in(keys[2], 2), own, number, ROWS_DEV * STEPS, EXPERTS, TOPK, MOST, 2))(route_ids_keys, route_ids_turns).reshape((TOKENS, STEPS, TOPK))
    gate_weights = jnp.clip(0.1 + 0.4 * jax.random.uniform(keys[3], (TOKENS, STEPS, TOPK), jnp.float32) ** steps_of(keys[3], (TOKENS, STEPS, TOPK), ((0, 128),), -0.2, 0.2), 0.1, 0.5)
    w_gate = noise(keys[4], (EXPERTS, D, FFH), D ** -0.5, 0.09375, ((0, 128),))
    w_up = noise(keys[5], (EXPERTS, D, FFH), D ** -0.5, 0.09375, ((0, 128),))
    w_down = noise(keys[6], (EXPERTS, FFH, D), FFH ** -0.5, 0.1875, ((0, 128),))
    return {"hidden": hidden, "norm_gain": norm_gain, "route_ids": route_ids, "gate_weights": gate_weights, "w_gate": w_gate, "w_up": w_up, "w_down": w_down}


def reference(hidden, norm_gain, route_ids, gate_weights, w_gate, w_up, w_down):
    widened = hidden.astype(jnp.float32)
    scale_rows = lax.rsqrt(lax.optimization_barrier(jnp.mean(widened * widened, axis=-1, keepdims=True)) + 1e-06)
    normed = (widened * scale_rows * norm_gain).astype(jnp.bfloat16)
    count = TOKENS * STEPS
    flat_rows = normed.reshape(count, D)
    flat_routes = route_ids.reshape(count, TOPK).astype(jnp.int32)
    flat_gates = gate_weights.reshape(count, TOPK).astype(jnp.float32)
    capacity = min(count, N_GRP * N_EP * MOST)

    def visit(total, pieces):
        gate_mat, up_mat, down_mat, expert = pieces
        hit = flat_routes == expert
        chosen = jnp.any(hit, axis=1)
        weight = lax.optimization_barrier(jnp.sum(jnp.where(hit, flat_gates, 0.0), axis=1))
        picked = jnp.nonzero(chosen, size=capacity, fill_value=0)[0].astype(jnp.int32)
        valid = jnp.arange(capacity, dtype=jnp.int32) < jnp.sum(chosen.astype(jnp.int32))
        rows = flat_rows[picked]
        gate_part = jnp.dot(rows, gate_mat, preferred_element_type=jnp.float32)
        up_part = jnp.dot(rows, up_mat, preferred_element_type=jnp.float32)
        act = (jax.nn.silu(gate_part) * up_part).astype(jnp.bfloat16)
        produced = jnp.dot(act, down_mat, preferred_element_type=jnp.float32).astype(jnp.bfloat16)
        factor = jnp.where(valid, weight[picked], 0.0)
        total = total.at[picked].add(produced.astype(jnp.float32) * factor[:, None])
        return (total, None)
    start = jnp.zeros((count, D), jnp.float32)
    experts_ids = jnp.arange(EXPERTS, dtype=jnp.int32)
    total, _ = lax.scan(visit, start, (w_gate, w_up, w_down, experts_ids))
    return total.reshape(TOKENS, STEPS, D).astype(jnp.bfloat16)
```

```python
import functools

import jax
import jax.numpy as jnp
from jax import lax
from jax.experimental import pallas as pl
from jax.experimental.pallas import tpu as pltpu
from jax.sharding import PartitionSpec as P

MESH = pl.DeviceIdType.MESH
F32 = jnp.float32
BF16 = jnp.bfloat16
ORDERS = (("y", "z", "x"), ("z", "x", "y"), ("x", "y", "z"))
STRIDE = {"x": 2, "y": 32, "z": 8}
RANGE = 4
ROWS = 16
META = 128


def part_widths(dmodel):
    tiles = dmodel // 256
    small = tiles // 3
    rest = tiles - small
    return (small * 256, rest // 2 * 256, (rest - rest // 2) * 256)


def device(coords):
    return (coords["y"], coords["z"] * 8 + coords["x"] * 2 + coords["core"])


def aligned(start, size):
    return pl.ds(pl.multiple_of(start, ROWS), size)


def iota(shape, dim):
    return lax.broadcasted_iota(jnp.int32, shape, dim)


def arrival_index(t, i):
    x, core, z, y, rank = i // 64, i // 32 % 2, i // 8 % 4, i // 2 % 4, i % 2
    at = {"x": x, "y": y, "z": z}
    a, b, c = ORDERS[t]
    return at[c] * 64 + core * 32 + at[b] * 8 + at[a] * 2 + rank


def kernel(
    widths,
    hid_ref,
    gain_ref,
    ig_ref,
    flat_ref,
    wg_hbm,
    wu_hbm,
    wd_hbm,
    out_ref,
    wg,
    wu,
    wd,
    xs,
    sb,
    ar,
    perm,
    perm_t,
    gates,
    gate_acc,
    up_acc,
    act,
    ob,
    bk,
    pb,
    r2,
    pb2,
    r1,
    w_sem,
    send_sem,
    p1_sem,
    p2a_sem,
    p2b_sem,
    p3_sem,
    own_sem,
    r3_sem,
    r2_sem,
    r1_sem,
):
    ep = lax.axis_index("ep")
    me = {"y": lax.axis_index("grp"), "z": ep // 8, "x": ep // 2 % 4, "core": ep % 2}
    offs = [sum(widths[:t]) for t in range(3)]

    def moved(axis, step, core=0):
        other = dict(me)
        other[axis] = (me[axis] + step) % RANGE
        other["core"] = (me["core"] + core) % 2
        return other

    barrier = pltpu.get_barrier_semaphore()
    partners = [moved(ax, s, c) for ax in "xyz" for s in (1, 2, 3) for c in (0, 1)] + [moved("x", 0, 1)]
    for other in partners:
        pl.semaphore_signal(barrier, inc=1, device_id=device(other), device_id_type=MESH)

    loads = [
        pltpu.make_async_copy(src.at[0], dst, w_sem.at[n])
        for n, (src, dst) in enumerate(((wg_hbm, wg), (wu_hbm, wu), (wd_hbm, wd)))
    ]
    for load in loads:
        load.start()

    hid = hid_ref[...].astype(F32)
    scale = lax.rsqrt(jnp.mean(hid * hid, axis=-1, keepdims=True) + 1e-06)
    normed = (hid * scale * gain_ref[...]).astype(BF16)

    ig = ig_ref[...]
    lane, row = iota((ROWS, META), 1), iota((ROWS, META), 0)
    before = lane // 8 < row
    meta = jnp.where(lane < 16, ig, 0.0)
    for k in range(8):
        same = jnp.where(before & (ig[:, k : k + 1] == flat_ref[...]), 1.0, 0.0)
        rank = jnp.sum(same, axis=1, keepdims=True)
        meta = jnp.where(lane == k, 2.0 * ig + rank, meta)
    meta = meta.astype(BF16)

    for t in range(3):
        a, b, _ = ORDERS[t]
        mine = aligned((me[b] * 4 + me[a]) * ROWS, ROWS)
        xs[t][mine, : widths[t]] = normed[:, offs[t] : offs[t] + widths[t]]
        xs[t][mine, widths[t] :] = meta

    pl.semaphore_wait(barrier, len(partners))

    sends = []

    def send(src, dst, sem, other):
        copy = pltpu.make_async_remote_copy(
            src, dst, send_sem, sem, device_id=device(other), device_id_type=MESH
        )
        copy.start()
        sends.append(copy)

    def arrive(ref, sem):
        pltpu.make_async_copy(ref, ref, sem).wait()

    for t in range(3):
        a, b, _ = ORDERS[t]
        mine = xs[t].at[aligned((me[b] * 4 + me[a]) * ROWS, ROWS)]
        for step in (1, 3, 2):
            send(mine, mine, p1_sem.at[t], moved(a, step))

    for t in (1, 2):
        i, j = iota((256, 256), 0), iota((256, 256), 1)
        perm[t - 1] = jnp.where(arrival_index(t, i) == j, 1.0, 0.0).astype(BF16)
        perm_t[t - 1] = jnp.where(arrival_index(t, j) == i, 1.0, 0.0).astype(BF16)

    for t in range(3):
        a, b, _ = ORDERS[t]
        arrive(xs[t].at[pl.ds(0, 3 * ROWS)], p1_sem.at[t])
        mine = xs[t].at[aligned(me[b] * 64, 64)]
        pair = dict(me)
        pair[b] = me[b] + 1 - 2 * (me[b] % 2)
        send(mine, mine, p2a_sem.at[t], pair)
        across = dict(me)
        across[b] = (pair[b] + 2) % RANGE
        send(mine, mine, p2b_sem.at[t], across)
        send(mine, mine, p2b_sem.at[t], moved(b, 2))

    def slots(t, half):
        _, _, c = ORDERS[t]
        base = dict(me)
        base[c] = 0
        first = base["y"] * 32 + base["z"] * 8 + base["x"] * 2
        rows = aligned(half * 128, 128)
        info = xs[t][rows, widths[t] :].astype(F32).T
        i, j = iota((128, 128), 0), iota((128, 128), 1)
        expert = first + i // 32 * STRIDE[c] + i // 16 % 2
        code = (expert * 2 + i % 2).astype(F32)
        hit = jnp.zeros((128, 128), F32)
        for k in range(8):
            hit = jnp.where(info[k : k + 1, :] == code, 1.0, hit)
        hit = jnp.where(j // 16 == i % 16 // 2, hit, 0.0).astype(BF16)
        sb[t][half] = jnp.dot(hit, xs[t][rows, : widths[t]], preferred_element_type=F32).astype(BF16)
        spot = me[c] * 2 + me["core"]
        there = ar[t].at[aligned(spot * 32 + half * 16, 16)]
        for step in (1, 3, 2, 0):
            for core in (0, 1):
                other = moved(c, step, core)
                piece = sb[t].at[half, aligned((other[c] * 2 + other["core"]) * 16, 16)]
                if step == 0 and core == 0:
                    pltpu.make_async_copy(piece, there, own_sem.at[t]).start()
                else:
                    send(piece, there, p3_sem.at[t], other)

    for t in range(3):
        b = ORDERS[t][1]
        arrive(xs[t].at[pl.ds(0, 64)], p2a_sem.at[t])
        slots(t, me[b] // 2)
    for t in range(3):
        b = ORDERS[t][1]
        arrive(xs[t].at[pl.ds(0, 128)], p2b_sem.at[t])
        slots(t, 1 - me[b] // 2)

    for t in range(3):
        _, _, c = ORDERS[t]
        base = dict(me)
        base[c] = 0
        first = base["y"] * 32 + base["z"] * 8 + base["x"] * 2
        l = iota((64, 256), 1)
        code = ((first + l // 64 * STRIDE[c] + l // 32 % 2) * 2 + l % 2).astype(F32)
        for q in range(4):
            info = xs[t][q * 64 : (q + 1) * 64, widths[t] :].astype(F32)
            owner = q * 4 + iota((64, 256), 0) // 16
            weight = jnp.zeros((64, 256), F32)
            for k in range(8):
                weight = jnp.where(info[:, k : k + 1] == code, info[:, 8 + k : 9 + k], weight)
            weight = jnp.where(owner == l % 32 // 2, weight, 0.0)
            gates[t, q * 64 : (q + 1) * 64] = weight.astype(BF16)

    loads[0].wait()
    loads[1].wait()
    hidden_units = gate_acc.shape[1]
    for t in range(3):
        for _ in range(2):
            arrive(ar[t].at[pl.ds(0, 16)], own_sem.at[t])
        arrive(ar[t].at[pl.ds(0, 224)], p3_sem.at[t])
        if t > 0:
            ar[t][...] = jnp.dot(perm[t - 1], ar[t][...], preferred_element_type=F32).astype(BF16)
        depth = pl.ds(offs[t], widths[t])

        def tile(n, carry, t=t, depth=depth):
            cols = pl.ds(pl.multiple_of(n * 256, 256), 256)
            for weights, total in ((wg, gate_acc), (wu, up_acc)):
                part = jnp.dot(ar[t][...], weights[depth, cols], preferred_element_type=F32)
                total[:, cols] = part if t == 0 else total[:, cols] + part
            return carry

        lax.fori_loop(0, hidden_units // 256, tile, 0)

    gate = gate_acc[...]
    act[0] = (gate / (1.0 + jnp.exp(-gate)) * up_acc[...]).astype(BF16)

    loads[2].wait()
    for t in range(3):
        _, _, c = ORDERS[t]
        if t > 0:
            act[t] = jnp.dot(perm_t[t - 1], act[0], preferred_element_type=F32).astype(BF16)

        def tile(n, carry, t=t):
            cols = pl.ds(pl.multiple_of(n * 256, 256), 256)
            from_cols = pl.ds(pl.multiple_of(offs[t] + n * 256, 256), 256)
            ob[t][:, cols] = jnp.dot(act[t], wd[:, from_cols], preferred_element_type=F32).astype(BF16)
            return carry

        lax.fori_loop(0, widths[t] // 256, tile, 0)
        spot = me[c] * 2 + me["core"]
        there = bk[t].at[aligned(spot * 32, 32)]
        for step in (1, 3, 2, 0):
            for core in (0, 1):
                other = moved(c, step, core)
                piece = ob[t].at[aligned((other[c] * 2 + other["core"]) * 32, 32)]
                if step == 0 and core == 0:
                    pltpu.make_async_copy(piece, there, own_sem.at[t]).start()
                else:
                    send(piece, there, r3_sem.at[t], other)

    for t in range(3):
        _, b, _ = ORDERS[t]
        arrive(bk[t].at[pl.ds(0, 32)], own_sem.at[t])
        arrive(bk[t].at[pl.ds(0, 224)], r3_sem.at[t])
        pb[t][...] = jnp.dot(gates[t], bk[t][...], preferred_element_type=F32).astype(BF16)
        there = r2[t].at[aligned(me[b] * 64, 64)]
        for step in (1, 3, 2):
            other = moved(b, step)
            send(pb[t].at[aligned(other[b] * 64, 64)], there, r2_sem.at[t], other)
        mine = aligned(me[b] * 64, 64)
        r2[t][mine] = pb[t][mine]

    for t in range(3):
        a, _, _ = ORDERS[t]
        arrive(r2[t].at[pl.ds(0, 192)], r2_sem.at[t])
        total = r2[t][0:64].astype(F32)
        for n in range(1, 4):
            total = total + r2[t][n * 64 : (n + 1) * 64].astype(F32)
        pb2[t][...] = total.astype(BF16)
        there = r1[t].at[aligned(me[a] * 16, 16)]
        for step in (1, 3, 2):
            other = moved(a, step)
            send(pb2[t].at[aligned(other[a] * 16, 16)], there, r1_sem.at[t], other)
        mine = aligned(me[a] * 16, 16)
        r1[t][mine] = pb2[t][mine]

    for t in range(3):
        arrive(r1[t].at[pl.ds(0, 48)], r1_sem.at[t])
        total = r1[t][0:16].astype(F32)
        for n in range(1, 4):
            total = total + r1[t][n * 16 : (n + 1) * 16].astype(F32)
        out_ref[:, offs[t] : offs[t] + widths[t]] = total.astype(BF16)

    for copy in sends:
        copy.wait_send()


def body(hidden, norm_gain, route_ids, gate_weights, w_gate, w_up, w_down):
    rows, steps, dmodel = hidden.shape
    topk = route_ids.shape[2]
    units = w_gate.shape[2]
    widths = part_widths(dmodel)
    count = rows * steps
    ids = route_ids.reshape(count, topk).astype(F32)
    ig = jnp.concatenate([ids, gate_weights.reshape(count, topk)], axis=1)
    ig = jnp.pad(ig, ((0, 0), (0, META - 2 * topk)))

    def each(rows_of, extra=0):
        return [pltpu.VMEM((*rows_of, w + extra), BF16) for w in widths]

    vmem = pl.BlockSpec(memory_space=pltpu.VMEM)
    hbm = pl.BlockSpec(memory_space=pl.ANY)
    sem = pltpu.SemaphoreType.DMA
    result = pl.pallas_call(
        functools.partial(kernel, widths),
        out_shape=jax.ShapeDtypeStruct((count, dmodel), BF16),
        in_specs=[vmem] * 4 + [hbm] * 3,
        out_specs=vmem,
        scratch_shapes=[
            pltpu.VMEM((dmodel, units), BF16),
            pltpu.VMEM((dmodel, units), BF16),
            pltpu.VMEM((units, dmodel), BF16),
            each((256,), META),
            each((2, 128)),
            each((256,)),
            pltpu.VMEM((2, 256, 256), BF16),
            pltpu.VMEM((2, 256, 256), BF16),
            pltpu.VMEM((3, 256, 256), BF16),
            pltpu.VMEM((256, units), F32),
            pltpu.VMEM((256, units), F32),
            pltpu.VMEM((3, 256, units), BF16),
            each((256,)),
            each((256,)),
            each((256,)),
            each((256,)),
            each((64,)),
            each((64,)),
            sem((3,)),
            sem,
            sem((3,)),
            sem((3,)),
            sem((3,)),
            sem((3,)),
            sem((3,)),
            sem((3,)),
            sem((3,)),
            sem((3,)),
        ],
        compiler_params=pltpu.CompilerParams(
            collective_id=0, has_side_effects=True, vmem_limit_bytes=56 * 2**20
        ),
        cost_estimate=pl.CostEstimate(
            flops=6 * 256 * dmodel * units, bytes_accessed=6 * dmodel * units, transcendentals=256 * units
        ),
    )(
        hidden.reshape(count, dmodel),
        norm_gain.reshape(1, dmodel),
        ig,
        ids.reshape(1, count * topk),
        w_gate,
        w_up,
        w_down,
    )
    return result.reshape(rows, steps, dmodel)


def solution(mesh):
    split = P(("grp", "ep"), None, None)
    return jax.shard_map(
        body,
        mesh=mesh,
        in_specs=(split, P(), split, split, split, split, split),
        out_specs=split,
        check_vma=False,
    )
```

```python
import functools

import jax
import jax.numpy as jnp
from jax import lax
from jax.experimental import pallas as pl
from jax.experimental.pallas import tpu as pltpu
from jax.sharding import PartitionSpec as P

MESH = pl.DeviceIdType.MESH
F32 = jnp.float32
BF16 = jnp.bfloat16
ORDERS = (("y", "z", "x"), ("z", "x", "y"), ("x", "y", "z"))
STRIDE = {"x": 2, "y": 32, "z": 8}
RANGE = 4
ROWS = 16
META = 128
PLANE = 32
SLOTS = 8
UNITS = 2


PEERS = [(i, j, core) for i in (2, 1, 3, 0) for j in (2, 1, 3, 0) for core in (1, 0)][:-1]


def part_widths(dmodel):
    tiles, count = dmodel // 256, 3 * UNITS
    width = [tiles // count] * count
    for n in range(tiles % count):
        width[(n * 2 + n // 3) % count if UNITS > 1 else n] += 1
    return tuple(w * 256 for w in width)


def device(coords):
    return (coords["y"], coords["z"] * 8 + coords["x"] * 2 + coords["core"])


def aligned(start, size):
    return pl.ds(pl.multiple_of(start, ROWS), size)


def iota(shape, dim):
    return lax.broadcasted_iota(jnp.int32, shape, dim)


def arrival_index(t, i):
    z, x, core, y, rank = i // 64, i // 16 % 4, i // 8 % 2, i // 2 % 4, i % 2
    at = {"x": x, "y": y, "z": z}
    a, b, c = ORDERS[t]
    return at[b] * 64 + at[c] * 16 + core * 8 + at[a] * 2 + rank


def kernel(
    widths,
    hid_ref,
    gain_ref,
    ids_ref,
    gw_ref,
    wg_hbm,
    wu_hbm,
    wd_hbm,
    out_ref,
    wg,
    wu,
    wd,
    xs,
    sb,
    ar,
    perm,
    perm_t,
    hits_of,
    gates,
    gate_acc,
    up_acc,
    act,
    ob,
    bk,
    pf,
    pb,
    r1,
    w_sem,
    send_sem,
    p1_sem,
    p2_sem,
    r2_sem,
    r1_sem,
):
    ep = lax.axis_index("ep")
    me = {"y": lax.axis_index("grp"), "z": ep // 8, "x": ep // 2 % 4, "core": ep % 2}
    chunks = range(len(widths))
    offs = [sum(widths[:n]) for n in chunks]

    def moved(steps):
        other = dict(me)
        for axis, step in steps.items():
            other[axis] = (me[axis] + step) % (2 if axis == "core" else RANGE)
        return other

    barrier = pltpu.get_barrier_semaphore()
    steps = [
        {"x": x, "y": y, "z": z, "core": core}
        for x in range(4)
        for y in range(4)
        for z in range(4)
        for core in range(2)
        if (x, y, z).count(0) >= 2 and (x, y, z, core) != (0, 0, 0, 0)
    ]
    for step in steps:
        pl.semaphore_signal(barrier, inc=1, device_id=device(moved(step)), device_id_type=MESH)

    loads = [
        pltpu.make_async_copy(src.at[0], dst, w_sem.at[n])
        for n, (src, dst) in enumerate(((wg_hbm, wg), (wu_hbm, wu), (wd_hbm, wd)))
    ]
    for load in loads:
        load.start()

    hid = hid_ref[...].astype(F32).reshape(ROWS, hid_ref.shape[2])
    scale = lax.rsqrt(jnp.mean(hid * hid, axis=-1, keepdims=True) + 1e-06)
    normed = (hid * scale * gain_ref[...].reshape(1, gain_ref.shape[0])).astype(BF16)

    topk = ids_ref.shape[2]
    ids = ids_ref[...].astype(F32).reshape(ROWS, topk)
    gw = gw_ref[...].reshape(ROWS, topk)
    lane = iota((ROWS, META), 1)
    lane_f = lane.astype(F32)
    hits = jnp.zeros((ROWS, META), F32)
    for k in range(topk):
        hits = jnp.where(ids[:, k : k + 1] == lane_f, 1.0, hits)
    lower = jnp.where(iota((ROWS, ROWS), 1) < iota((ROWS, ROWS), 0), 1.0, 0.0).astype(BF16)
    earlier = jnp.dot(lower, hits.astype(BF16), preferred_element_type=F32)
    meta = jnp.zeros((ROWS, META), F32)
    for k in range(topk):
        own = ids[:, k : k + 1]
        rank = jnp.sum(jnp.where(own == lane_f, earlier, 0.0), axis=1, keepdims=True)
        meta = jnp.where(lane == k, 2.0 * own + rank, meta)
        meta = jnp.where(lane == topk + k, gw[:, k : k + 1], meta)
    meta = meta.astype(BF16)

    for n in chunks:
        mine = aligned(me[ORDERS[n % 3][0]] * ROWS, ROWS)
        xs[n][mine, : widths[n]] = normed[:, offs[n] : offs[n] + widths[n]]
        if n < 3:
            xs[n][mine, widths[n] :] = meta

    pl.semaphore_wait(barrier, len(steps))

    sends = []

    def send(src, dst, sem, other):
        copy = pltpu.make_async_remote_copy(
            src, dst, send_sem, sem, device_id=device(other), device_id_type=MESH
        )
        copy.start()
        sends.append(copy)

    def arrive(ref, sem):
        pltpu.make_async_copy(ref, ref, sem).wait()

    def place(t, coords):
        _, b, c = ORDERS[t]
        return coords[b] * 8 + coords[c] * 2 + coords["core"]

    def over_planes(first, src, dst, sem):
        for s0, s1, core in PEERS:
            for n in (first, first + 1, first + 2):
                _, b, c = ORDERS[n % 3]
                other = moved({b: s0, c: s1, "core": core})
                send(src[n].at[place(n % 3, other)], dst[n].at[place(n % 3, me)], sem.at[n], other)
        for n in (first, first + 1, first + 2):
            here = place(n % 3, me)
            dst[n][here] = src[n][here]

    for n in chunks:
        a = ORDERS[n % 3][0]
        mine = xs[n].at[aligned(me[a] * ROWS, ROWS)]
        for step in (1, 3, 2):
            send(mine, mine, p1_sem.at[n], moved({a: step}))

    for t in (1, 2):
        i, j = iota((256, 256), 0), iota((256, 256), 1)
        perm[t - 1] = jnp.where(arrival_index(t, i) == j, 1.0, 0.0).astype(BF16)
        perm_t[t - 1] = jnp.where(arrival_index(t, j) == i, 1.0, 0.0).astype(BF16)

    def slot_code(t, slot):
        _, b, c = ORDERS[t]
        base = dict(me)
        base[b], base[c] = 0, 0
        first = base["y"] * 32 + base["z"] * 8 + base["x"] * 2
        expert = first + slot // 64 * STRIDE[b] + slot // 16 % 4 * STRIDE[c] + slot // 8 % 2
        return (expert * 2 + slot % 2).astype(F32)

    for t in range(3):
        arrive(xs[t].at[pl.ds(0, 3 * ROWS)], p1_sem.at[t])
    for n in chunks:
        t = n % 3
        if n < 3:
            info = xs[t][:, widths[t] :].astype(F32).T
            slot, row = iota((256, 64), 0), iota((256, 64), 1)
            code = slot_code(t, slot)
            hit = jnp.zeros((256, 64), F32)
            for k in range(topk):
                hit = jnp.where(info[k : k + 1, :] == code, 1.0, hit)
            hits_of[t] = jnp.where(row // ROWS == slot % 8 // 2, hit, 0.0).astype(BF16)
        else:
            arrive(xs[n].at[pl.ds(0, 3 * ROWS)], p1_sem.at[n])
        picked = jnp.dot(hits_of[t], xs[n][:, : widths[n]], preferred_element_type=F32).astype(BF16)
        sb[n][...] = picked.reshape(PLANE, SLOTS, widths[n])
        if t == 2:
            over_planes(n - 2, sb, ar, p2_sem)

    for t in range(3):
        info = xs[t][:, widths[t] :].astype(F32)
        row, slot = iota((64, 256), 0), iota((64, 256), 1)
        code = slot_code(t, slot)
        weight = jnp.zeros((64, 256), F32)
        for k in range(topk):
            weight = jnp.where(info[:, k : k + 1] == code, info[:, topk + k : topk + k + 1], weight)
        gates[t] = jnp.where(row // ROWS == slot % 8 // 2, weight, 0.0).astype(BF16)

    loads[0].wait()
    loads[1].wait()
    units = gate_acc.shape[1]
    for n in chunks:
        arrive(ar[n].at[pl.ds(0, PLANE - 1)], p2_sem.at[n])
        rows = ar[n][...].reshape(PLANE * SLOTS, widths[n])
        if n % 3 > 0:
            rows = jnp.dot(perm[n % 3 - 1], rows, preferred_element_type=F32).astype(BF16)
        depth = pl.ds(offs[n], widths[n])
        for first in range(0, units, 512):
            cols = pl.ds(first, 512)
            for weights, total in ((wg, gate_acc), (wu, up_acc)):
                part = jnp.dot(rows, weights[depth, cols], preferred_element_type=F32)
                total[:, cols] = part if n == 0 else total[:, cols] + part

    gate = gate_acc[...]
    act[0] = (gate / (1.0 + jnp.exp(-gate)) * up_acc[...]).astype(BF16)

    loads[2].wait()
    for n in chunks:
        t = n % 3
        if n in (1, 2):
            act[t] = jnp.dot(perm_t[t - 1], act[0], preferred_element_type=F32).astype(BF16)
        for first in range(0, widths[n], 256):
            cols = pl.ds(offs[n] + first, 256)
            made = jnp.dot(act[t], wd[:, cols], preferred_element_type=F32).astype(BF16)
            ob[n][:, :, first : first + 256] = made.reshape(PLANE, SLOTS, 256)
        if t == 2:
            over_planes(n - 2, ob, bk, r2_sem)

    for n in chunks:
        a = ORDERS[n % 3][0]
        arrive(bk[n].at[pl.ds(0, PLANE - 1)], r2_sem.at[n])
        back = bk[n][...].reshape(PLANE * SLOTS, widths[n])
        pf[n][...] = jnp.dot(gates[n % 3], back, preferred_element_type=F32)
        pb[n][...] = pf[n][...].astype(BF16)
        there = r1[n].at[aligned(me[a] * ROWS, ROWS)]
        for step in (1, 3, 2):
            other = moved({a: step})
            send(pb[n].at[aligned(other[a] * ROWS, ROWS)], there, r1_sem.at[n], other)
        r1[n][aligned(me[a] * ROWS, ROWS)] = jnp.zeros((ROWS, widths[n]), BF16)

    for n in chunks:
        a = ORDERS[n % 3][0]
        arrive(r1[n].at[pl.ds(0, 3 * ROWS)], r1_sem.at[n])
        total = pf[n][aligned(me[a] * ROWS, ROWS)]
        for k in range(4):
            total = total + r1[n][k * ROWS : (k + 1) * ROWS].astype(F32)
        out_ref[:, :, offs[n] : offs[n] + widths[n]] = total.reshape(ROWS // 2, 2, widths[n]).astype(BF16)

    for copy in sends:
        copy.wait_send()


def body(hidden, norm_gain, route_ids, gate_weights, w_gate, w_up, w_down):
    rows, steps, dmodel = hidden.shape
    topk = route_ids.shape[2]
    units = w_gate.shape[2]
    widths = part_widths(dmodel)
    count = rows * steps

    def each(rows_of, extra=0, kind=BF16):
        return [pltpu.VMEM((*rows_of, w + extra * (n < 3)), kind) for n, w in enumerate(widths)]

    vmem = pl.BlockSpec(memory_space=pltpu.VMEM)
    hbm = pl.BlockSpec(memory_space=pl.ANY)
    sem = pltpu.SemaphoreType.DMA
    result = pl.pallas_call(
        functools.partial(kernel, widths),
        out_shape=jax.ShapeDtypeStruct(hidden.shape, BF16),
        in_specs=[vmem] * 4 + [hbm] * 3,
        out_specs=vmem,
        scratch_shapes=[
            pltpu.VMEM((dmodel, units), BF16),
            pltpu.VMEM((dmodel, units), BF16),
            pltpu.VMEM((units, dmodel), BF16),
            each((64,), META),
            each((PLANE, SLOTS)),
            each((PLANE, SLOTS)),
            pltpu.VMEM((2, 256, 256), BF16),
            pltpu.VMEM((2, 256, 256), BF16),
            pltpu.VMEM((3, 256, 64), BF16),
            pltpu.VMEM((3, 64, 256), BF16),
            pltpu.VMEM((256, units), F32),
            pltpu.VMEM((256, units), F32),
            pltpu.VMEM((3, 256, units), BF16),
            each((PLANE, SLOTS)),
            each((PLANE, SLOTS)),
            each((64,), kind=F32),
            each((64,)),
            each((64,)),
            sem((3,)),
            sem,
        ]
        + [sem((len(widths),))] * 4,
        compiler_params=pltpu.CompilerParams(
            collective_id=0, has_side_effects=True, vmem_limit_bytes=56 * 2**20
        ),
        cost_estimate=pl.CostEstimate(
            flops=6 * 256 * dmodel * units, bytes_accessed=6 * dmodel * units, transcendentals=256 * units
        ),
    )(
        hidden,
        norm_gain,
        route_ids,
        gate_weights,
        w_gate,
        w_up,
        w_down,
    )
    return result


def solution(mesh):
    split = P(("grp", "ep"), None, None)
    return jax.shard_map(
        body,
        mesh=mesh,
        in_specs=(split, P(), split, split, split, split, split),
        out_specs=split,
        check_vma=False,
    )
```

```python
import functools

import jax
import jax.numpy as jnp
from jax import lax
from jax.experimental import pallas as pl
from jax.experimental.pallas import tpu as pltpu
from jax.sharding import PartitionSpec as P

MESH = pl.DeviceIdType.MESH
F32 = jnp.float32
BF16 = jnp.bfloat16
ORDERS = (("y", "z", "x"), ("z", "x", "y"), ("x", "y", "z"))
STRIDE = {"x": 2, "y": 32, "z": 8}
RANGE = 4
ROWS = 16
META = 128
PLANE = 16
SLOTS = 8
HALF = PLANE * SLOTS
PEERS = [(i, j) for i in (2, 1, 3, 0) for j in (2, 1, 3, 0)]


def part_widths(dmodel):
    tiles = dmodel // 128
    small = tiles // 3
    rest = tiles - small
    return ((rest - rest // 2) * 128, rest // 2 * 128, small * 128)


def device(coords):
    return (coords["y"], coords["z"] * 8 + coords["x"] * 2 + coords["core"])


def aligned(start, size):
    return pl.ds(pl.multiple_of(start, ROWS), size)


def iota(shape, dim):
    return lax.broadcasted_iota(jnp.int32, shape, dim)


def arrival_index(t, i):
    z, x, y, rank = i // 32, i // 8 % 4, i // 2 % 4, i % 2
    at = {"x": x, "y": y, "z": z}
    a, b, c = ORDERS[t]
    return at[b] * 32 + at[c] * 8 + at[a] * 2 + rank


def kernel(
    widths,
    hid_hbm,
    gain_hbm,
    ids_hbm,
    gw_hbm,
    wg_hbm,
    wu_hbm,
    wd_hbm,
    out_hbm,
    hid_ref,
    gain_ref,
    ids_ref,
    gw_ref,
    out_ref,
    wg,
    wu,
    wd,
    xs,
    sb,
    ar,
    perm,
    perm_t,
    gates,
    gate_acc,
    up_acc,
    act,
    ob,
    bk,
    pf,
    pb,
    r1,
    io_sem,
    w_sem,
    send_sem,
    p1_sem,
    p2_sem,
    r2_sem,
    r1_sem,
):
    ep = lax.axis_index("ep")
    me = {"y": lax.axis_index("grp"), "z": ep // 8, "x": ep // 2 % 4, "core": ep % 2}
    parts = range(3)
    offs = [sum(widths[:t]) for t in parts]

    def moved(steps):
        other = dict(me)
        for axis, step in steps.items():
            other[axis] = (me[axis] + step) % (2 if axis == "core" else RANGE)
        return other

    barrier = pltpu.get_barrier_semaphore()
    steps = [
        {"x": x, "y": y, "z": z, "core": core}
        for x in range(4)
        for y in range(4)
        for z in range(4)
        for core in range(2)
        if (x, y, z).count(0) >= 2 and (x, y, z, core) != (0, 0, 0, 0)
    ]
    for step in steps:
        pl.semaphore_signal(barrier, inc=1, device_id=device(moved(step)), device_id_type=MESH)

    inputs = [
        pltpu.make_async_copy(src, dst, io_sem.at[n])
        for n, (src, dst) in enumerate(
            ((hid_hbm, hid_ref), (gain_hbm, gain_ref), (ids_hbm, ids_ref), (gw_hbm, gw_ref))
        )
    ]
    for load in inputs:
        load.start()

    loads = [
        pltpu.make_async_copy(src.at[0], dst, w_sem.at[n])
        for n, (src, dst) in enumerate(((wg_hbm, wg), (wu_hbm, wu), (wd_hbm, wd)))
    ]
    for load in inputs:
        load.wait()
    for load in loads:
        load.start()
    hid = hid_ref[...].astype(F32).reshape(ROWS, hid_ref.shape[2])
    scale = lax.rsqrt(jnp.mean(hid * hid, axis=-1, keepdims=True) + 1e-06)
    normed = (hid * scale * gain_ref[...].reshape(1, gain_ref.shape[0])).astype(BF16)

    topk = ids_ref.shape[2]
    ids = ids_ref[...].astype(F32).reshape(ROWS, topk)
    gw = gw_ref[...].reshape(ROWS, topk)
    lane = iota((ROWS, META), 1)
    lane_f = lane.astype(F32)
    hits = jnp.zeros((ROWS, META), F32)
    for k in range(topk):
        hits = jnp.where(ids[:, k : k + 1] == lane_f, 1.0, hits)
    lower = jnp.where(iota((ROWS, ROWS), 1) < iota((ROWS, ROWS), 0), 1.0, 0.0).astype(BF16)
    earlier = jnp.dot(lower, hits.astype(BF16), preferred_element_type=F32)
    meta = jnp.zeros((ROWS, META), F32)
    for k in range(topk):
        own = ids[:, k : k + 1]
        rank = jnp.sum(jnp.where(own == lane_f, earlier, 0.0), axis=1, keepdims=True)
        meta = jnp.where(lane == k, 2.0 * own + rank, meta)
        meta = jnp.where(lane == topk + k, gw[:, k : k + 1], meta)
    meta = meta.astype(BF16)

    for t in parts:
        mine = aligned(me[ORDERS[t][0]] * ROWS, ROWS)
        xs[t][mine, : widths[t]] = normed[:, offs[t] : offs[t] + widths[t]]
        xs[t][mine, widths[t] :] = meta

    pl.semaphore_wait(barrier, len(steps))

    sends = []

    def send(src, dst, sem, other):
        copy = pltpu.make_async_remote_copy(
            src, dst, send_sem, sem, device_id=device(other), device_id_type=MESH
        )
        copy.start()
        sends.append(copy)

    def arrive(ref, sem):
        pltpu.make_async_copy(ref, ref, sem).wait()

    def place(t, coords):
        _, b, c = ORDERS[t]
        return coords[b] * 4 + coords[c]

    def over_plane(half, t, src, dst, sem):
        _, b, c = ORDERS[t]
        here = place(t, me)
        for s0, s1 in PEERS:
            if (s0, s1, half) != (0, 0, 0):
                other = moved({b: s0, c: s1, "core": half})
                send(src.at[place(t, other)], dst.at[here], sem, other)
        if half == 0:
            dst[here] = src[here]

    def arrive_plane(half, ref, sem):
        arrive(ref.at[pl.ds(0, PLANE - 1 + half)], sem)

    for t in parts:
        a = ORDERS[t][0]
        mine = xs[t].at[aligned(me[a] * ROWS, ROWS)]
        for step in (1, 3, 2):
            send(mine, mine, p1_sem.at[t], moved({a: step}))

    for t in (1, 2):
        i, j = iota((HALF, HALF), 0), iota((HALF, HALF), 1)
        perm[t - 1] = jnp.where(arrival_index(t, i) == j, 1.0, 0.0).astype(BF16)
        perm_t[t - 1] = jnp.where(arrival_index(t, j) == i, 1.0, 0.0).astype(BF16)

    def slot_code(half, t, slot):
        _, b, c = ORDERS[t]
        base = dict(me)
        base[b], base[c] = 0, 0
        first = base["y"] * 32 + base["z"] * 8 + base["x"] * 2 + (base["core"] + half) % 2
        expert = first + slot // 32 * STRIDE[b] + slot // 8 % 4 * STRIDE[c]
        return (expert * 2 + slot % 2).astype(F32)

    def slots(half, t):
        rows = xs[t]
        info = rows[:, widths[t] :].astype(F32).T
        slot, row = iota((HALF, 64), 0), iota((HALF, 64), 1)
        code = slot_code(half, t, slot)
        hit = jnp.zeros((HALF, 64), F32)
        for k in range(topk):
            hit = jnp.where(info[k : k + 1, :] == code, 1.0, hit)
        hit = jnp.where(row // ROWS == slot % 8 // 2, hit, 0.0).astype(BF16)
        picked = jnp.dot(hit, rows[:, : widths[t]], preferred_element_type=F32).astype(BF16)
        n = half * 3 + t
        sb[n][...] = picked.reshape(PLANE, SLOTS, widths[t])
        over_plane(half, t, sb[n], ar[n], p2_sem.at[n])

    def weights_back(half, t):
        info = xs[t][:, widths[t] :].astype(F32)
        row, slot = iota((64, HALF), 0), iota((64, HALF), 1)
        code = slot_code(half, t, slot)
        weight = jnp.zeros((64, HALF), F32)
        for k in range(topk):
            weight = jnp.where(info[:, k : k + 1] == code, info[:, topk + k : topk + k + 1], weight)
        gates[half * 3 + t] = jnp.where(row // ROWS == slot % 8 // 2, weight, 0.0).astype(BF16)

    for t in parts:
        arrive(xs[t].at[pl.ds(0, 3 * ROWS)], p1_sem.at[t])
    for half in (0, 1):
        for t in parts:
            slots(half, t)
    for half in (0, 1):
        for t in parts:
            weights_back(half, t)

    units = gate_acc.shape[1]
    for half in (0, 1):
        if half == 0:
            loads[0].wait()
            loads[1].wait()
        for t in parts:
            n = half * 3 + t
            arrive_plane(half, ar[n], p2_sem.at[n])
            rows = ar[n][...].reshape(HALF, widths[t])
            if t > 0:
                rows = jnp.dot(perm[t - 1], rows, preferred_element_type=F32).astype(BF16)
            depth = pl.ds(offs[t], widths[t])
            for first in range(0, units, 512):
                cols = pl.ds(first, 512)
                for weights, total in ((wg, gate_acc), (wu, up_acc)):
                    part = jnp.dot(rows, weights[depth, cols], preferred_element_type=F32)
                    total[:, cols] = part if t == 0 else total[:, cols] + part

        gate = gate_acc[...]
        act[0] = (gate / (1.0 + jnp.exp(-gate)) * up_acc[...]).astype(BF16)

        if half == 0:
            loads[2].wait()
        for t in parts:
            n = half * 3 + t
            if t > 0:
                act[t] = jnp.dot(perm_t[t - 1], act[0], preferred_element_type=F32).astype(BF16)
            for first in range(0, widths[t], 256):
                wide = min(256, widths[t] - first)
                cols = pl.ds(offs[t] + first, wide)
                made = jnp.dot(act[t], wd[:, cols], preferred_element_type=F32).astype(BF16)
                ob[n][:, :, first : first + wide] = made.reshape(PLANE, SLOTS, wide)
            over_plane(half, t, ob[n], bk[n], r2_sem.at[n])

    for half in (0, 1):
        for t in parts:
            a = ORDERS[t][0]
            n = half * 3 + t
            arrive_plane(half, bk[n], r2_sem.at[n])
            back = bk[n][...].reshape(HALF, widths[t])
            summed = jnp.dot(gates[n], back, preferred_element_type=F32)
            if half == 0:
                pf[t][...] = summed
            else:
                summed = pf[t][...] + summed
                pf[t][...] = summed
                pb[t][...] = summed.astype(BF16)
                for step in (2, 1, 3):
                    other = moved({a: step})
                    send(pb[t].at[aligned(other[a] * ROWS, ROWS)], r1[t].at[step - 1], r1_sem.at[t], other)

    stores = []
    for t in parts:
        a = ORDERS[t][0]
        arrive(r1[t], r1_sem.at[t])
        total = pf[t][aligned(me[a] * ROWS, ROWS)]
        for k in range(3):
            total = total + r1[t][k].astype(F32)
        cols = pl.ds(offs[t], widths[t])
        out_ref[:, :, cols] = total.reshape(ROWS // 2, 2, widths[t]).astype(BF16)
        stores.append(pltpu.make_async_copy(out_ref.at[:, :, cols], out_hbm.at[:, :, cols], io_sem.at[t]))
        stores[-1].start()

    for store in stores:
        store.wait()
    for copy in sends:
        copy.wait_send()


def body(hidden, norm_gain, route_ids, gate_weights, w_gate, w_up, w_down):
    rows, steps, dmodel = hidden.shape
    topk = route_ids.shape[2]
    units = w_gate.shape[2]
    widths = part_widths(dmodel)
    count = rows * steps

    def each(rows_of, extra=0, kind=BF16, halves=2):
        return [pltpu.VMEM((*rows_of, w + extra), kind) for w in widths * halves]

    hbm = pl.BlockSpec(memory_space=pl.ANY)
    sem = pltpu.SemaphoreType.DMA
    result = pl.pallas_call(
        functools.partial(kernel, widths),
        out_shape=jax.ShapeDtypeStruct(hidden.shape, BF16),
        in_specs=[hbm] * 7,
        out_specs=hbm,
        scratch_shapes=[
            pltpu.VMEM(hidden.shape, BF16),
            pltpu.VMEM(norm_gain.shape, F32),
            pltpu.VMEM(route_ids.shape, jnp.int32),
            pltpu.VMEM(gate_weights.shape, F32),
            pltpu.VMEM(hidden.shape, BF16),
            pltpu.VMEM((dmodel, units), BF16),
            pltpu.VMEM((dmodel, units), BF16),
            pltpu.VMEM((units, dmodel), BF16),
            each((64,), META, halves=1),
            each((PLANE, SLOTS)),
            each((PLANE, SLOTS)),
            pltpu.VMEM((2, HALF, HALF), BF16),
            pltpu.VMEM((2, HALF, HALF), BF16),
            pltpu.VMEM((6, 64, HALF), BF16),
            pltpu.VMEM((HALF, units), F32),
            pltpu.VMEM((HALF, units), F32),
            pltpu.VMEM((3, HALF, units), BF16),
            each((PLANE, SLOTS)),
            each((PLANE, SLOTS)),
            each((64,), kind=F32, halves=1),
            each((64,), halves=1),
            each((3, ROWS), halves=1),
            sem((4,)),
            sem((3,)),
            sem,
            sem((3,)),
            sem((6,)),
            sem((6,)),
            sem((3,)),
        ],
        compiler_params=pltpu.CompilerParams(
            collective_id=0, has_side_effects=True, vmem_limit_bytes=56 * 2**20
        ),
        cost_estimate=pl.CostEstimate(
            flops=6 * 256 * dmodel * units, bytes_accessed=6 * dmodel * units, transcendentals=256 * units
        ),
    )(
        hidden,
        norm_gain,
        route_ids,
        gate_weights,
        w_gate,
        w_up,
        w_down,
    )
    return result


def solution(mesh):
    split = P(("grp", "ep"), None, None)
    return jax.shard_map(
        body,
        mesh=mesh,
        in_specs=(split, P(), split, split, split, split, split),
        out_specs=split,
        check_vma=False,
    )
```

```python
import functools

import jax
import jax.numpy as jnp
from jax import lax
from jax.experimental import pallas as pl
from jax.experimental.pallas import tpu as pltpu
from jax.sharding import PartitionSpec as P

MESH = pl.DeviceIdType.MESH
F32 = jnp.float32
BF16 = jnp.bfloat16
ORDERS = (("y", "z", "x"), ("z", "x", "y"), ("x", "y", "z"))
STRIDE = {"x": 2, "y": 32, "z": 8}
RANGE = 4
ROWS = 16
META = 128
PLANE = 16
SLOTS = 8
HALF = PLANE * SLOTS
SPLIT = ((1, 2),)
PEERS = [(i, j) for i in (2, 1, 3, 0) for j in (2, 1, 3, 0)]


def part_widths(dmodel):
    tiles = dmodel // 128
    small = tiles // 3
    rest = tiles - small
    return ((rest - rest // 2) * 128, rest // 2 * 128, small * 128)


def device(coords):
    return (coords["y"], coords["z"] * 8 + coords["x"] * 2 + coords["core"])


def aligned(start, size):
    return pl.ds(pl.multiple_of(start, ROWS), size)


def iota(shape, dim):
    return lax.broadcasted_iota(jnp.int32, shape, dim)


def arrival_index(t, i):
    z, x, y, rank = i // 32, i // 8 % 4, i // 2 % 4, i % 2
    at = {"x": x, "y": y, "z": z}
    a, b, c = ORDERS[t]
    return at[b] * 32 + at[c] * 8 + at[a] * 2 + rank


def kernel(
    widths,
    hid_hbm,
    gain_hbm,
    ids_hbm,
    gw_hbm,
    wg_hbm,
    wu_hbm,
    wd_hbm,
    out_hbm,
    hid_ref,
    gain_ref,
    ids_ref,
    gw_ref,
    out_ref,
    wg,
    wu,
    wd,
    xs,
    sb,
    ar,
    perm,
    perm_t,
    gates,
    gate_acc,
    up_acc,
    act,
    ob,
    bk,
    pf,
    pb,
    r1,
    io_sem,
    w_sem,
    send_sem,
    p1_sem,
    p2_sem,
    r2_sem,
    r1_sem,
    out_sem,
):
    ep = lax.axis_index("ep")
    me = {"y": lax.axis_index("grp"), "z": ep // 8, "x": ep // 2 % 4, "core": ep % 2}
    parts = range(3)
    sign = 1 + 2 * me["core"]
    offs = [sum(widths[:t]) for t in parts]

    def moved(steps):
        other = dict(me)
        for axis, step in steps.items():
            other[axis] = (me[axis] + step) % (2 if axis == "core" else RANGE)
        return other

    barrier = pltpu.get_barrier_semaphore()
    steps = [
        {"x": x, "y": y, "z": z, "core": core}
        for x in range(4)
        for y in range(4)
        for z in range(4)
        for core in range(2)
        if (x, y, z).count(0) >= 2 and (x, y, z, core) != (0, 0, 0, 0)
    ]
    for step in steps:
        pl.semaphore_signal(barrier, inc=1, device_id=device(moved(step)), device_id_type=MESH)

    inputs = [
        pltpu.make_async_copy(src, dst, io_sem.at[n])
        for n, (src, dst) in enumerate(
            ((hid_hbm, hid_ref), (gain_hbm, gain_ref), (ids_hbm, ids_ref), (gw_hbm, gw_ref))
        )
    ]
    for load in inputs:
        load.start()

    loads = [
        pltpu.make_async_copy(src.at[0], dst, w_sem.at[n])
        for n, (src, dst) in enumerate(((wg_hbm, wg), (wu_hbm, wu), (wd_hbm, wd)))
    ]
    for load in inputs:
        load.wait()
    for load in loads:
        load.start()
    hid = hid_ref[...].astype(F32).reshape(ROWS, hid_ref.shape[2])
    scale = lax.rsqrt(jnp.mean(hid * hid, axis=-1, keepdims=True) + 1e-06)
    normed = (hid * scale * gain_ref[...].reshape(1, gain_ref.shape[0])).astype(BF16)

    topk = ids_ref.shape[2]
    ids = ids_ref[...].astype(F32).reshape(ROWS, topk)
    gw = gw_ref[...].reshape(ROWS, topk)
    lane = iota((ROWS, META), 1)
    lane_f = lane.astype(F32)
    hits = jnp.zeros((ROWS, META), F32)
    for k in range(topk):
        hits = jnp.where(ids[:, k : k + 1] == lane_f, 1.0, hits)
    lower = jnp.where(iota((ROWS, ROWS), 1) < iota((ROWS, ROWS), 0), 1.0, 0.0).astype(BF16)
    earlier = jnp.dot(lower, hits.astype(BF16), preferred_element_type=F32)
    meta = jnp.zeros((ROWS, META), F32)
    for k in range(topk):
        own = ids[:, k : k + 1]
        rank = jnp.sum(jnp.where(own == lane_f, earlier, 0.0), axis=1, keepdims=True)
        meta = jnp.where(lane == k, 2.0 * own + rank, meta)
        meta = jnp.where(lane == topk + k, gw[:, k : k + 1], meta)
    meta = meta.astype(BF16)

    for t in parts:
        mine = aligned(me[ORDERS[t][0]] * ROWS, ROWS)
        xs[t][mine, : widths[t]] = normed[:, offs[t] : offs[t] + widths[t]]
        xs[t][mine, widths[t] :] = meta

    pl.semaphore_wait(barrier, len(steps))

    sends = []

    def send(src, dst, sem, other):
        copy = pltpu.make_async_remote_copy(
            src, dst, send_sem, sem, device_id=device(other), device_id_type=MESH
        )
        copy.start()
        sends.append(copy)

    def arrive(ref, sem):
        pltpu.make_async_copy(ref, ref, sem).wait()

    def place(t, coords):
        _, b, c = ORDERS[t]
        return coords[b] * 4 + coords[c]

    def pieces(half, t):
        if (half, t) in SPLIT:
            first = (widths[t] // 2 + 64) // 128 * 128
            return [(0, first), (first, widths[t] - first)]
        return [(0, widths[t])]

    def over_plane(half, t, src, dst, sem):
        _, b, c = ORDERS[t]
        here = place(t, me)
        for s0, s1 in PEERS:
            if (s0, s1, half) != (0, 0, 0):
                other = moved({b: s0 * sign, c: s1 * sign, "core": half})
                send(src.at[place(t, other)], dst.at[here], sem, other)
        if half == 0:
            dst[here] = src[here]

    def arrive_plane(half, ref, sem):
        arrive(ref.at[pl.ds(0, PLANE - 1 + half)], sem)

    for t in parts:
        a = ORDERS[t][0]
        mine = xs[t].at[aligned(me[a] * ROWS, ROWS)]
        for step in (1, 3, 2):
            send(mine, mine, p1_sem.at[t], moved({a: step}))

    for t in (1, 2):
        i, j = iota((HALF, HALF), 0), iota((HALF, HALF), 1)
        perm[t - 1] = jnp.where(arrival_index(t, i) == j, 1.0, 0.0).astype(BF16)
        perm_t[t - 1] = jnp.where(arrival_index(t, j) == i, 1.0, 0.0).astype(BF16)

    def slot_code(half, t, slot):
        _, b, c = ORDERS[t]
        base = dict(me)
        base[b], base[c] = 0, 0
        first = base["y"] * 32 + base["z"] * 8 + base["x"] * 2 + (base["core"] + half) % 2
        expert = first + slot // 32 * STRIDE[b] + slot // 8 % 4 * STRIDE[c]
        return (expert * 2 + slot % 2).astype(F32)

    def slots(half, t):
        rows = xs[t]
        info = rows[:, widths[t] :].astype(F32).T
        slot, row = iota((HALF, 64), 0), iota((HALF, 64), 1)
        code = slot_code(half, t, slot)
        hit = jnp.zeros((HALF, 64), F32)
        for k in range(topk):
            hit = jnp.where(info[k : k + 1, :] == code, 1.0, hit)
        hit = jnp.where(row // ROWS == slot % 8 // 2, hit, 0.0).astype(BF16)
        picked = jnp.dot(hit, rows[:, : widths[t]], preferred_element_type=F32).astype(BF16)
        n = half * 3 + t
        sb[n][...] = picked.reshape(PLANE, SLOTS, widths[t])
        over_plane(half, t, sb[n], ar[n], p2_sem.at[n])

    def weights_back(half, t):
        info = xs[t][:, widths[t] :].astype(F32)
        row, slot = iota((64, HALF), 0), iota((64, HALF), 1)
        code = slot_code(half, t, slot)
        weight = jnp.zeros((64, HALF), F32)
        for k in range(topk):
            weight = jnp.where(info[:, k : k + 1] == code, info[:, topk + k : topk + k + 1], weight)
        gates[half * 3 + t] = jnp.where(row // ROWS == slot % 8 // 2, weight, 0.0).astype(BF16)

    for t in parts:
        arrive(xs[t].at[pl.ds(0, 3 * ROWS)], p1_sem.at[t])
    for half in (0, 1):
        for t in parts:
            slots(half, t)
    for half in (0, 1):
        for t in parts:
            weights_back(half, t)

    units = gate_acc.shape[1]
    for half in (0, 1):
        if half == 0:
            loads[0].wait()
            loads[1].wait()
        for t in parts:
            n = half * 3 + t
            arrive_plane(half, ar[n], p2_sem.at[n])
            rows = ar[n][...].reshape(HALF, widths[t])
            if t > 0:
                rows = jnp.dot(perm[t - 1], rows, preferred_element_type=F32).astype(BF16)
            depth = pl.ds(offs[t], widths[t])
            for first in range(0, units, 512):
                cols = pl.ds(first, 512)
                for weights, total in ((wg, gate_acc), (wu, up_acc)):
                    part = jnp.dot(rows, weights[depth, cols], preferred_element_type=F32)
                    total[:, cols] = part if t == 0 else total[:, cols] + part

        gate = gate_acc[...]
        act[0] = (gate / (1.0 + jnp.exp(-gate)) * up_acc[...]).astype(BF16)

        if half == 0:
            loads[2].wait()
        for t in parts:
            n = half * 3 + t
            if t > 0:
                act[t] = jnp.dot(perm_t[t - 1], act[0], preferred_element_type=F32).astype(BF16)
            for q, (left, size) in enumerate(pieces(half, t)):
                for first in range(left, left + size, 256):
                    wide = min(256, left + size - first)
                    cols = pl.ds(offs[t] + first, wide)
                    made = jnp.dot(act[t], wd[:, cols], preferred_element_type=F32).astype(BF16)
                    ob[n][:, :, first : first + wide] = made.reshape(PLANE, SLOTS, wide)
                cols = pl.ds(left, size)
                over_plane(half, t, ob[n].at[:, :, cols], bk[n].at[:, :, cols], r2_sem.at[n, q])

    for half in (0, 1):
        for t in parts:
            a = ORDERS[t][0]
            n = half * 3 + t
            for q, (left, size) in enumerate(pieces(half, t)):
                cols = pl.ds(left, size)
                arrive_plane(half, bk[n].at[:, :, cols], r2_sem.at[n, q])
                back = bk[n][:, :, cols].reshape(HALF, size)
                summed = jnp.dot(gates[n], back, preferred_element_type=F32)
                if half == 0:
                    pf[t][:, cols] = summed
                else:
                    summed = pf[t][:, cols] + summed
                    pf[t][:, cols] = summed
                    pb[t][:, cols] = summed.astype(BF16)
                    for step in (2, 1, 3):
                        other = moved({a: step})
                        src = pb[t].at[aligned(other[a] * ROWS, ROWS), cols]
                        send(src, r1[t].at[step - 1, :, cols], r1_sem.at[t, q], other)

    stores = []
    for t in parts:
        a = ORDERS[t][0]
        for q, (left, size) in enumerate(pieces(1, t)):
            cols = pl.ds(left, size)
            arrive(r1[t].at[:, :, cols], r1_sem.at[t, q])
            total = pf[t][aligned(me[a] * ROWS, ROWS), cols]
            for k in range(3):
                total = total + r1[t][k, :, cols].astype(F32)
            there = pl.ds(offs[t] + left, size)
            out_ref[:, :, there] = total.reshape(ROWS // 2, 2, size).astype(BF16)
            stores.append(
                pltpu.make_async_copy(out_ref.at[:, :, there], out_hbm.at[:, :, there], out_sem.at[t, q])
            )
            stores[-1].start()

    for store in stores:
        store.wait()
    for copy in sends:
        copy.wait_send()


def body(hidden, norm_gain, route_ids, gate_weights, w_gate, w_up, w_down):
    rows, steps, dmodel = hidden.shape
    topk = route_ids.shape[2]
    units = w_gate.shape[2]
    widths = part_widths(dmodel)
    count = rows * steps

    def each(rows_of, extra=0, kind=BF16, halves=2):
        return [pltpu.VMEM((*rows_of, w + extra), kind) for w in widths * halves]

    hbm = pl.BlockSpec(memory_space=pl.ANY)
    sem = pltpu.SemaphoreType.DMA
    result = pl.pallas_call(
        functools.partial(kernel, widths),
        out_shape=jax.ShapeDtypeStruct(hidden.shape, BF16),
        in_specs=[hbm] * 7,
        out_specs=hbm,
        scratch_shapes=[
            pltpu.VMEM(hidden.shape, BF16),
            pltpu.VMEM(norm_gain.shape, F32),
            pltpu.VMEM(route_ids.shape, jnp.int32),
            pltpu.VMEM(gate_weights.shape, F32),
            pltpu.VMEM(hidden.shape, BF16),
            pltpu.VMEM((dmodel, units), BF16),
            pltpu.VMEM((dmodel, units), BF16),
            pltpu.VMEM((units, dmodel), BF16),
            each((64,), META, halves=1),
            each((PLANE, SLOTS)),
            each((PLANE, SLOTS)),
            pltpu.VMEM((2, HALF, HALF), BF16),
            pltpu.VMEM((2, HALF, HALF), BF16),
            pltpu.VMEM((6, 64, HALF), BF16),
            pltpu.VMEM((HALF, units), F32),
            pltpu.VMEM((HALF, units), F32),
            pltpu.VMEM((3, HALF, units), BF16),
            each((PLANE, SLOTS)),
            each((PLANE, SLOTS)),
            each((64,), kind=F32, halves=1),
            each((64,), halves=1),
            each((3, ROWS), halves=1),
            sem((4,)),
            sem((3,)),
            sem,
            sem((3,)),
            sem((6,)),
            sem((6, 2)),
            sem((3, 2)),
            sem((3, 2)),
        ],
        compiler_params=pltpu.CompilerParams(
            collective_id=0, has_side_effects=True, vmem_limit_bytes=56 * 2**20
        ),
        cost_estimate=pl.CostEstimate(
            flops=6 * 256 * dmodel * units, bytes_accessed=6 * dmodel * units, transcendentals=256 * units
        ),
    )(
        hidden,
        norm_gain,
        route_ids,
        gate_weights,
        w_gate,
        w_up,
        w_down,
    )
    return result


def solution(mesh):
    split = P(("grp", "ep"), None, None)
    return jax.shard_map(
        body,
        mesh=mesh,
        in_specs=(split, P(), split, split, split, split, split),
        out_specs=split,
        check_vma=False,
    )
```
